512 devices in a mesh: dp: 32 (over x, z_lo), leaf: 16 (over y, z_hi, core).
Axes of the slice: x: 4, y: 4, z: 16 (z_hi: 2, z_lo: 8; z = z_hi * 8 + z_lo), core: 2. Of those that a mesh axis runs over, the one named last changes fastest.
Arguments:
- hidden: bfloat16 [512, 128, 5120], P(('dp', 'leaf')), may hold values from -6 to 6
- queries: bfloat16 [512, 128, 4096], P(('dp', 'leaf')), may hold values from -80 to 80
- key_value_weight: bfloat16 [5120, 1024], P('dp'), may hold values from -0.078125 to 0.078125
- k_gain: float32 [128], replicated, may hold values from 0.1 to 1.9
- cached_ancestor_keys: bfloat16 [32, 16, 128, 512], P('dp', 'leaf'), may hold values from -6 to 6
- cached_ancestor_values: bfloat16 [32, 16, 128, 512], P('dp', 'leaf'), may hold values from -6 to 6
- ancestor_mask: int32 [512, 16], P(('dp', 'leaf')), may hold values from 0 to 1, as said below
- fork_offset: int32 [512], P(('dp', 'leaf')), may hold values from 0 to 2047
Outputs:
- attended: bfloat16 [512, 128, 4096], P(('dp', 'leaf'))
The draws below stay inside these ranges and needn't reach their ends.
Inputs may be any that keep to these rules, and one draw needn't show every extreme that they name: `ancestor_mask`: for each branch the ones form one run of consecutive blocks whose last is block fork_offset // 128.
All inputs are finite; a program needn't handle non-finite values.
Results may differ from the reference program's by a relative error of at most 0.0057.
Values may be sent and summed in bfloat16 or wider, within the bound.
No kernel may reach another device: no remote copies, remote signals or barrier semaphores. Data moves between devices by JAX's collectives and lax.ppermute only.
A program may use at most 64 MiB of HBM per device.

```python
import jax
import jax.numpy as jnp
from jax import lax

MODEL_WIDTH = 5120
QUERY_HEADS = 32
KEY_HEADS = 4
HEAD_SIZE = 128
BLOCK_TOKENS = 128
SEGMENT_TOKENS = 128
BRANCHES = 512
ANCESTOR_COUNT = 16
N_DP = 32


def tree_layout(key):
    first = jax.random.randint(jax.random.fold_in(key, 101), (BRANCHES,), 0, ANCESTOR_COUNT)
    last = jax.random.randint(jax.random.fold_in(key, 102), (BRANCHES,), first, ANCESTOR_COUNT)
    inner = jax.random.randint(jax.random.fold_in(key, 103), (BRANCHES,), 0, BLOCK_TOKENS)
    last = last.at[0].set(ANCESTOR_COUNT - 1)
    inner = inner.at[0].set(BLOCK_TOKENS - 1)
    first = first.at[1].set(0)
    last = last.at[1].set(0)
    inner = inner.at[1].set(0)
    blocks = jnp.arange(ANCESTOR_COUNT, dtype=jnp.int32)
    mask = ((blocks[None, :] >= first[:, None]) & (blocks[None, :] <= last[:, None])).astype(jnp.int32)
    return (mask, last * BLOCK_TOKENS + inner)


def draw_queries(key, part):
    key = jax.random.fold_in(key, 11)
    target_shape = (BRANCHES, SEGMENT_TOKENS, QUERY_HEADS * HEAD_SIZE)
    return jnp.clip(2.0 * jax.random.normal(key, target_shape, jnp.float32), -8.0, 8.0).astype(jnp.bfloat16)


def draw_cached_ancestor_keys(key, part):
    key = jax.random.fold_in(key, 12)
    target_shape = (N_DP, ANCESTOR_COUNT, BLOCK_TOKENS, KEY_HEADS * HEAD_SIZE)
    return jnp.clip(jax.random.normal(key, target_shape, jnp.float32), -5.0, 5.0).astype(jnp.bfloat16)


def draw_ancestor_mask(key, part):
    mask, fork = tree_layout(key)
    return mask


def draw_fork_offset(key, part):
    mask, fork = tree_layout(key)
    return fork


def steps_of(stream_key, extent, pieces, least, high):
    factor_of = 1.0
    for dim, shards_of in pieces:
        steps = jax.random.uniform(jax.random.fold_in(jax.random.fold_in(stream_key, 6), dim), (shards_of,), jnp.float32, least / len(pieces), high / len(pieces))
        factor_of = factor_of * jnp.repeat(jnp.exp(steps), extent[dim] // shards_of).reshape((-1,) + (1,) * (len(extent) - 1 - dim))
    return factor_of


def scatter_about(rng, extent, deviation, reach, shards=(), held_as=jnp.bfloat16):
    gain = steps_of(rng, extent, shards, -0.22, 0.18) if shards else 1.0
    entries = jax.random.normal(rng, extent, jnp.float32) * deviation * gain
    return jnp.minimum(jnp.maximum(entries, -reach), reach).astype(held_as)


def setup_inputs(seed: int = 0) -> dict:
    keys = jax.random.split(jax.random.key(seed), 9)
    hidden = scatter_about(keys[0], (BRANCHES, SEGMENT_TOKENS, MODEL_WIDTH), 1.0, 6.0, ((0, 512),))
    queries = draw_queries(jax.random.fold_in(keys[8], 71), 0)
    key_value_weight = scatter_about(keys[2], (MODEL_WIDTH, 2 * KEY_HEADS * HEAD_SIZE), MODEL_WIDTH ** -0.5, 0.078125, ((0, 32),))
    k_gain = jnp.clip(1.0 + 0.18 * jax.random.normal(keys[3], (HEAD_SIZE,), jnp.float32), 0.1, 1.9)
    cached_ancestor_keys = draw_cached_ancestor_keys(jax.random.fold_in(keys[8], 71), 0)
    cached_ancestor_values = scatter_about(keys[5], (N_DP, ANCESTOR_COUNT, BLOCK_TOKENS, KEY_HEADS * HEAD_SIZE), 1.0, 6.0, ((0, 32), (1, 16)))
    ancestor_mask = draw_ancestor_mask(jax.random.fold_in(keys[8], 71), 0)
    fork_offset = draw_fork_offset(jax.random.fold_in(keys[8], 71), 0)
    return dict(hidden=hidden, queries=queries, key_value_weight=key_value_weight, k_gain=k_gain, cached_ancestor_keys=cached_ancestor_keys, cached_ancestor_values=cached_ancestor_values, ancestor_mask=ancestor_mask, fork_offset=fork_offset)


EPS = 1e-06
THETA = 1000000.0

def rotate_keys(segment_keys, positions):
    half = segment_keys.shape[-1] // 2
    freq = THETA ** (-jnp.arange(half, dtype=jnp.float32) * 2.0 / segment_keys.shape[-1])
    angle = positions.astype(jnp.float32)[..., None] * freq
    cosine = jnp.cos(angle)[..., None, :]
    sine = jnp.sin(angle)[..., None, :]
    first = segment_keys[..., :half]
    second = segment_keys[..., half:]
    return jnp.concatenate([first * cosine - second * sine, second * cosine + first * sine], axis=-1)

def reference(hidden, queries, key_value_weight, k_gain, cached_ancestor_keys, cached_ancestor_values, ancestor_mask, fork_offset):
    key_value_width = KEY_HEADS * HEAD_SIZE
    query_groups = QUERY_HEADS // KEY_HEADS
    ancestor_length = ANCESTOR_COUNT * BLOCK_TOKENS
    scale = HEAD_SIZE ** (-0.5)
    positions_all = jnp.arange(ancestor_length, dtype=jnp.int32)
    causal = jnp.arange(SEGMENT_TOKENS)[:, None] >= jnp.arange(SEGMENT_TOKENS)[None, :]
    batch_rows = jnp.arange(BRANCHES, dtype=jnp.int32) // (BRANCHES // N_DP)

    def one_branch(items):
        query_rows, state, mask, fork, rollout_row = items
        expanded = jnp.repeat(mask, BLOCK_TOKENS)
        visible = (expanded == 1) & (positions_all <= fork)
        start = jnp.sum(visible.astype(jnp.int32))
        projected_rows = jnp.dot(state, key_value_weight, preferred_element_type=jnp.float32)
        segment_keys = projected_rows[:, :key_value_width].reshape(SEGMENT_TOKENS, KEY_HEADS, HEAD_SIZE)
        segment_keys = segment_keys * lax.rsqrt(lax.optimization_barrier(jnp.mean(segment_keys * segment_keys, axis=-1, keepdims=True)) + EPS) * k_gain
        segment_keys = rotate_keys(segment_keys, start + jnp.arange(SEGMENT_TOKENS, dtype=jnp.int32)).astype(jnp.bfloat16)
        segment_values = projected_rows[:, key_value_width:].reshape(SEGMENT_TOKENS, KEY_HEADS, HEAD_SIZE).astype(jnp.bfloat16)
        segment_keys, segment_values = lax.optimization_barrier((segment_keys, segment_values))
        prior_keys = lax.dynamic_index_in_dim(cached_ancestor_keys, rollout_row, 0, keepdims=False).reshape(ancestor_length, KEY_HEADS, HEAD_SIZE)
        prior_values = lax.dynamic_index_in_dim(cached_ancestor_values, rollout_row, 0, keepdims=False).reshape(ancestor_length, KEY_HEADS, HEAD_SIZE)
        all_keys = jnp.concatenate([prior_keys, segment_keys], axis=0).astype(jnp.float32)
        all_values = jnp.concatenate([prior_values, segment_values], axis=0).astype(jnp.float32)
        grouped_queries = query_rows.reshape(SEGMENT_TOKENS, KEY_HEADS, query_groups, HEAD_SIZE).astype(jnp.float32)
        scores = jnp.einsum('sgjd,lgd->gjsl', grouped_queries, all_keys) * scale
        allowed = jnp.concatenate([jnp.broadcast_to(visible[None, :], (SEGMENT_TOKENS, ancestor_length)), causal], axis=1)
        scores = jnp.where(allowed, scores, -jnp.inf)
        top = lax.optimization_barrier(jnp.max(scores, axis=-1, keepdims=True))
        weights = jnp.exp(scores - top)
        total = lax.optimization_barrier(jnp.sum(weights, axis=-1))
        rounded = lax.optimization_barrier(weights.astype(jnp.bfloat16)).astype(jnp.float32)
        summed = jnp.einsum('gjsl,lgd->sgjd', rounded, all_values)
        summed = summed / jnp.transpose(total, (2, 0, 1))[..., None]
        return summed.reshape(SEGMENT_TOKENS, QUERY_HEADS * HEAD_SIZE).astype(jnp.bfloat16)
    return lax.map(one_branch, (queries, hidden, ancestor_mask, fork_offset, batch_rows))
```

```python
import functools
import math

import jax
import jax.numpy as jnp
from jax import lax
from jax.experimental import pallas as pl
from jax.experimental.pallas import tpu as pltpu
from jax.sharding import PartitionSpec as P

EPS = 1e-06
THETA = 1000000.0
HEAD = 128
TOK = 128
FLOOR = -1e30
EXP_SCALE = HEAD ** (-0.5) * math.log2(math.e)
AXES = ("dp", "leaf")
NX, NZL, NY, NZH = 4, 8, 4, 2
NZ = NZL * NZH
BF = jnp.bfloat16
F32 = jnp.float32
VMEM = pl.BlockSpec(memory_space=pltpu.VMEM)
SMEM = pl.BlockSpec(memory_space=pltpu.SMEM)
HBM = pl.BlockSpec(memory_space=pltpu.HBM)
VMEM_LIMIT = 36 * 2**20
CORE, Y, ZH, X, ZL = range(5)
FIRST, SECOND = (0, 4, 2, 6), (1, 5, 3, 7)
ROUND_Y = (0, 2, 1, 3)


def place(x, y, z, core):
    return ((x % NX * NZL + z % NZL) * NY + y % NY) * 4 + (z // NZL % NZH) * 2 + core


def move(a, x=0, y=0, z=0, ways=(1, -1)):
    pairs = []
    for px in range(NX):
        for pz in range(NZ):
            for py in range(NY):
                for core, way in enumerate(ways):
                    to = place(px + way * x, py + way * y, (pz + way * z) % NZ, core)
                    pairs.append((place(px, py, pz, core), to))
    return lax.ppermute(a, AXES, pairs)


def swap_cores(a):
    pairs = [(n, n ^ 1) for n in range(NX * NY * NZ * 2)]
    return lax.ppermute(a, AXES, pairs)


def together(*arrays):
    return lax.optimization_barrier(arrays)


def dot_nt(a, b):
    return lax.dot_general(a, b, (((1,), (1,)), ((), ())), preferred_element_type=F32)


def run_copies(pairs, sems):
    copies = [pltpu.make_async_copy(a, b, sems.at[n]) for n, (a, b) in enumerate(pairs)]
    for copy in copies:
        copy.start()
    for copy in copies:
        copy.wait()


def columns(ref, start, size):
    return ref.at[:, pl.ds(pl.multiple_of(start, HEAD), size)]


def load_kernel(coord_ref, w_ref, k_ref, v_ref, load_ref):
    core = coord_ref[CORE]
    half = w_ref.shape[1] // 4
    shard = w_ref.shape[0]
    for n in range(2):
        start = pl.multiple_of((2 * n + core) * half, HEAD)
        load_ref[:shard, n * half : (n + 1) * half] = w_ref[:, pl.ds(start, half)]
    load_ref[shard : shard + TOK, :] = k_ref[...]
    load_ref[shard + TOK :, :] = v_ref[...]


def pick_load(coords, w, k, v):
    return pl.pallas_call(
        load_kernel,
        out_shape=jax.ShapeDtypeStruct((w.shape[0] + 2 * TOK, w.shape[1] // 2), BF),
        in_specs=[SMEM, VMEM, VMEM, VMEM],
        out_specs=VMEM,
        name="pick_load",
    )(coords, w, k, v)


def part_kernel(away, coord_ref, load_ref, hidden_ref, unit_ref, *part_refs):
    first = load_ref.shape[0] - 2 * TOK
    for n in range(2):
        unit_ref[n] = load_ref[first + n * TOK : first + (n + 1) * TOK, :]
    part = hidden_ref.shape[1] // NX
    for dx, ref in zip(away, part_refs):
        start = pl.multiple_of(lax.rem(coord_ref[X] + dx, NX) * part, HEAD)
        ref[...] = hidden_ref[:, pl.ds(start, part)]


def pick_parts(coords, load, hidden, away):
    part = jax.ShapeDtypeStruct((TOK, hidden.shape[1] // NX), BF)
    return pl.pallas_call(
        functools.partial(part_kernel, away),
        out_shape=(jax.ShapeDtypeStruct((2, TOK, load.shape[1]), BF),) + (part,) * len(away),
        in_specs=[SMEM, VMEM, VMEM],
        out_specs=(VMEM,) * (1 + len(away)),
        cost_estimate=pl.CostEstimate(flops=10**11, bytes_accessed=1000, transcendentals=0),
        name="pick_parts",
    )(coords, load, hidden)


def project_kernel(coord_ref, hidden_ref, *refs):
    peers, refs = refs[: NX - 1], refs[NX - 1 :]
    bundles, refs = refs[:4], refs[4:]
    own_ref, backs, (h_buf, w_buf, sems) = refs[0], refs[1:NX], refs[NX:]
    core, x, zl = coord_ref[CORE], coord_ref[X], coord_ref[ZL]
    part = h_buf.shape[1]
    pairs = [(columns(hidden_ref, x * part, part), h_buf.at[pl.ds(0, TOK)])]
    for n, ref in enumerate(peers):
        pairs.append((ref, h_buf.at[pl.ds((n + 1) * TOK, TOK)]))
    shard = part // NZL
    for ref, offsets, swapped in zip(bundles, (FIRST, SECOND) * 2, (0, 0, 1, 1)):
        from_core = 1 - core if swapped else core
        way = 1 - 2 * from_core
        for n, dz in enumerate(offsets):
            start = pl.multiple_of(lax.rem(zl - way * dz + NZL, NZL) * shard, 16)
            pairs.append((ref.at[pl.ds(n * shard, shard)], w_buf.at[from_core, pl.ds(start, shard)]))
    run_copies(pairs, sems)
    half = w_buf.shape[2] // 2
    keys = 2 * half
    for side in range(2):
        product = jnp.dot(h_buf[...], w_buf[side], preferred_element_type=F32)
        k, v = product[:, :half], product[:, half:]
        own_ref[:, side * half : (side + 1) * half] = k[:TOK]
        own_ref[:, keys + side * half : keys + (side + 1) * half] = v[:TOK]
        for n, ref in enumerate(backs):
            rows = slice((n + 1) * TOK, (n + 2) * TOK)
            high = k[rows].astype(BF)
            low = (k[rows] - high.astype(F32)).astype(BF)
            for i, value in enumerate((high, low, v[rows].astype(BF))):
                ref[:, i * keys + side * half : i * keys + (side + 1) * half] = value


def project(coords, hidden, peers, bundles):
    part = peers[0].shape[1]
    width = bundles[0].shape[1]
    back = jax.ShapeDtypeStruct((TOK, 3 * width), BF)
    return pl.pallas_call(
        project_kernel,
        out_shape=(jax.ShapeDtypeStruct((TOK, 2 * width), F32),) + (back,) * (NX - 1),
        in_specs=[SMEM] + [HBM] * (1 + len(peers) + len(bundles)),
        out_specs=(VMEM,) * NX,
        scratch_shapes=[
            pltpu.VMEM((NX * TOK, part), BF),
            pltpu.VMEM((2, part, width), BF),
            pltpu.SemaphoreType.DMA((NX + 2 * NZL,)),
        ],
        compiler_params=pltpu.CompilerParams(vmem_limit_bytes=VMEM_LIMIT),
        cost_estimate=pl.CostEstimate(flops=10**11, bytes_accessed=1000, transcendentals=0),
        name="project",
    )(coords, hidden, *peers, *bundles)


def pack_kernel(*refs):
    at = 0
    for ref in refs[:-1]:
        refs[-1][at : at + ref.shape[0]] = ref[...]
        at += ref.shape[0]


def pack(blocks, rank):
    return pl.pallas_call(
        pack_kernel,
        out_shape=jax.ShapeDtypeStruct((sum(a.shape[0] for a in blocks), *blocks[0].shape[1:]), BF),
        in_specs=[VMEM] * len(blocks),
        out_specs=VMEM,
        cost_estimate=pl.CostEstimate(flops=rank, bytes_accessed=1000, transcendentals=0),
        name="pack",
    )(*blocks)


def seen_tokens(mask_ref, fork_ref, block):
    count = jnp.clip(fork_ref[0] + 1 - block * TOK, 0, TOK)
    return jnp.where(mask_ref[0, block] == 1, count, 0)


def attention_kernel(stage, together_heads, coord_ref, mask_ref, fork_ref, q_ref, *refs):
    segment, carried = stage == 2, stage > 0
    if segment:
        (cos_ref, sin_ref, gain_ref, own_ref), refs = refs[:4], refs[4:]
        backs, refs = refs[: NX - 1], refs[NX - 1 :]
    elif stage == 0:
        blocks, refs = [*(refs[0].at[n] for n in range(NY)), *refs[1 : NY + 1]], refs[NY + 1 :]
    else:
        blocks, refs = [refs[0].at[n] for n in range(2 * NY)], refs[1:]
    if carried:
        (acc_in, top_in, total_in), refs = refs[:3], refs[3:]
    if segment:
        out_ref, refs = refs[0], refs[1:]
    else:
        (acc_ref, top_ref, total_ref), refs = refs[:3], refs[3:]
    k_buf, v_buf = refs
    groups = k_buf.shape[0]
    heads = q_ref.shape[1] // HEAD
    per_group = heads // groups

    def lanes_of(h):
        return slice(h * HEAD, (h + 1) * HEAD)

    for g in range(groups):
        v_buf[g, :, HEAD:] = jnp.ones((k_buf.shape[1], HEAD), BF)
        if segment:
            k, v = own_ref[:, lanes_of(g)], own_ref[:, lanes_of(groups + g)]
            for ref in backs:
                high, low = ref[:, lanes_of(g)], ref[:, lanes_of(groups + g)]
                k = k + (high.astype(F32) + low.astype(F32))
                v = v + ref[:, lanes_of(2 * groups + g)].astype(F32)
            k = k * lax.rsqrt(jnp.mean(k * k, axis=1, keepdims=True) + EPS) * gain_ref[...]
            k = k * cos_ref[...] + pltpu.roll(k, HEAD // 2, 1) * sin_ref[...]
            k_buf[g] = k.astype(BF)
            v_buf[g, :, :HEAD] = v.astype(BF)
        else:
            for i, ref in enumerate(blocks):
                rows = slice(i * TOK, (i + 1) * TOK)
                k_buf[g, rows, :] = ref[0, :, lanes_of(g)]
                v_buf[g, rows, :HEAD] = ref[1, :, lanes_of(g)]
    if segment:
        row = lax.broadcasted_iota(jnp.int32, (TOK, TOK), 0)
        column = lax.broadcasted_iota(jnp.int32, (TOK, TOK), 1)
        bias = jnp.where(row >= column, 0.0, FLOOR)
        bias = jnp.concatenate([bias] * together_heads, axis=0)
    else:
        core, y, zh = coord_ref[CORE], coord_ref[Y], coord_ref[ZH]
        from_core = core if stage == 0 else 1 - core
        lane = lax.broadcasted_iota(jnp.int32, (1, TOK), 1)
        bias = []
        for side in (zh, 1 - zh):
            for away in ROUND_Y:
                block = lax.rem(y - away + NY, NY) * 4 + side * 2 + from_core
                bias.append(jnp.where(lane < seen_tokens(mask_ref, fork_ref, block), 0.0, FLOOR))
        bias = jnp.concatenate(bias, axis=1)
    units = [range(h, h + together_heads) for h in range(0, heads, together_heads)]

    def score(unit):
        q = jnp.concatenate([q_ref[:, lanes_of(h)] for h in unit], axis=0)
        return dot_nt(q, k_buf[unit[0] // per_group])

    ahead = score(units[0])
    for n, unit in enumerate(units):
        scores = ahead + bias
        if n + 1 < len(units):
            ahead = score(units[n + 1])
        top = jnp.max(scores, axis=1, keepdims=True)
        if carried:
            old = jnp.concatenate([top_in[:, lanes_of(h)] for h in unit], axis=0)
            wide = jnp.maximum(old, top)
            factor = jnp.exp2((old - wide) * EXP_SCALE)
            top = jnp.concatenate([wide] * (scores.shape[1] // HEAD), axis=1)
        else:
            wide = jnp.broadcast_to(top, (top.shape[0], HEAD))
        weights = jnp.exp2((scores - top) * EXP_SCALE).astype(BF)
        summed = jnp.dot(weights, v_buf[unit[0] // per_group], preferred_element_type=F32)
        for i, h in enumerate(unit):
            rows = slice(i * TOK, (i + 1) * TOK)
            value, total = summed[rows, :HEAD], summed[rows, HEAD:]
            if carried:
                value = value + acc_in[:, lanes_of(h)] * factor[rows]
                total = total + total_in[:, lanes_of(h)] * factor[rows]
            if segment:
                out_ref[:, lanes_of(h)] = (value / total).astype(BF)
            else:
                acc_ref[:, lanes_of(h)] = value
                top_ref[:, lanes_of(h)] = wide[rows]
                total_ref[:, lanes_of(h)] = total


def attention(stage, coords, mask, fork, queries, groups, operands):
    width = queries.shape[1]
    heads = width // HEAD
    length = TOK if stage == 2 else 2 * NY * TOK
    if stage == 2:
        out_shape = jax.ShapeDtypeStruct((TOK, width), BF)
    else:
        out_shape = (jax.ShapeDtypeStruct((TOK, width), F32),) * 3
    return pl.pallas_call(
        functools.partial(attention_kernel, stage, 4 if stage == 2 else 2),
        out_shape=out_shape,
        in_specs=[SMEM] * 3 + [VMEM] * (1 + len(operands)),
        out_specs=VMEM if stage == 2 else (VMEM,) * 3,
        scratch_shapes=[
            pltpu.VMEM((groups, length, HEAD), BF),
            pltpu.VMEM((groups, length, 2 * HEAD), BF),
        ],
        compiler_params=pltpu.CompilerParams(vmem_limit_bytes=VMEM_LIMIT),
        cost_estimate=pl.CostEstimate(flops=10**9, bytes_accessed=1000, transcendentals=0),
        name=("own_blocks", "other_blocks", "segment_block")[stage],
    )(coords, mask, fork, queries, *operands)


def on_device(
    hidden,
    queries,
    key_value_weight,
    k_gain,
    cached_ancestor_keys,
    cached_ancestor_values,
    ancestor_mask,
    fork_offset,
):
    dp, leaf = lax.axis_index("dp"), lax.axis_index("leaf")
    coords = jnp.stack([leaf % 2, leaf // 4, (leaf // 2) % 2, dp // NZL, dp % NZL]).astype(jnp.int32)
    groups = cached_ancestor_keys.shape[3] // HEAD
    keys, values = cached_ancestor_keys[0, 0], cached_ancestor_values[0, 0]
    load = pick_load(coords, key_value_weight, keys, values)
    unit, *sent = pick_parts(coords, load, hidden[0], (1,))

    block_start = jnp.arange(ancestor_mask.shape[1], dtype=jnp.int32) * TOK
    seen = jnp.clip(fork_offset[:, None] + 1 - block_start[None, :], 0, TOK)
    start = jnp.sum(jnp.where(ancestor_mask == 1, seen, 0))
    positions = (start + jnp.arange(TOK, dtype=jnp.int32)).astype(F32)
    freq = THETA ** (-jnp.arange(HEAD // 2, dtype=F32) * 2.0 / HEAD)
    angle = positions[:, None] * freq
    cosine, sine = jnp.cos(angle), jnp.sin(angle)
    cosine = jnp.concatenate([cosine, cosine], axis=-1)
    sine = jnp.concatenate([-sine, sine], axis=-1)

    def direct(a, **by):
        return move(a, ways=(1, 1), **by)

    def to_y_peers(a):
        return [direct(a, y=n) for n in ROUND_Y[1:]]

    shard = key_value_weight.shape[0]
    got = move(load, z=4)
    fours = jnp.concatenate([load[:shard], got[:shard]], axis=0)
    fours, far, part_one, *near = together(
        fours, got[shard:].reshape(unit.shape), direct(sent[0], x=1), *to_y_peers(unit)
    )
    _, *sent = pick_parts(coords, got, hidden[0], (2, 3))
    far, two, part_two, part_three, cosine, sine = together(
        move(far, z=4), move(fours, z=2), direct(sent[0], x=2), direct(sent[1], x=3), cosine, sine
    )
    first = jnp.concatenate([fours, two], axis=0)
    second, other_first = together(move(first, z=1), swap_cores(first))
    other_second = swap_cores(second)
    peers = [part_one, part_two, part_three]
    partial, *backs = project(coords, hidden[0], peers, [first, second, other_first, other_second])
    backs = [direct(backs[n - 1], x=-n) for n in (2, 3, 1)]
    near = pack([unit, *near], 10**13)
    far = [far, *to_y_peers(far)]
    other = swap_cores(pack([near, *far], 10**6)).reshape(2 * NY, *unit.shape)
    blocks = [near.reshape(NY, *unit.shape), *far]

    given = (coords, ancestor_mask, fork_offset, queries[0], groups)
    state = attention(0, *given, blocks)
    state = attention(1, *given, [other, *state])
    result = attention(2, *given, [cosine, sine, k_gain[None, :], partial, *backs, *state])
    return result[None]


def solution(mesh):
    in_specs = (
        P(("dp", "leaf"), None, None),
        P(("dp", "leaf"), None, None),
        P("dp", None),
        P(),
        P("dp", "leaf", None, None),
        P("dp", "leaf", None, None),
        P(("dp", "leaf"), None),
        P(("dp", "leaf")),
    )
    out_specs = P(("dp", "leaf"), None, None)
    return jax.shard_map(
        on_device, mesh=mesh, in_specs=in_specs, out_specs=out_specs, check_vma=False
    )
```

```python
import functools
import math

import jax
import jax.numpy as jnp
from jax import lax
from jax.experimental import pallas as pl
from jax.experimental.pallas import tpu as pltpu
from jax.sharding import PartitionSpec as P

EPS = 1e-06
THETA = 1000000.0
HEAD = 128
TOK = 128
FLOOR = -1e30
EXP_SCALE = HEAD ** (-0.5) * math.log2(math.e)
AXES = ("dp", "leaf")
NX, NZL, NY, NZH = 4, 8, 4, 2
NZ = NZL * NZH
BF = jnp.bfloat16
F32 = jnp.float32
VMEM = pl.BlockSpec(memory_space=pltpu.VMEM)
SMEM = pl.BlockSpec(memory_space=pltpu.SMEM)
HBM = pl.BlockSpec(memory_space=pltpu.HBM)
VMEM_LIMIT = 36 * 2**20
SMALL_LIMIT = 24 * 2**20
CORE, Y, ZH, X, ZL = range(5)
FIRST, SECOND = (0, 4, 2, 6), (1, 5, 3, 7)
ROUND_Y = (0, 2, 1, 3)


def place(x, y, z, core):
    return ((x % NX * NZL + z % NZL) * NY + y % NY) * 4 + (z // NZL % NZH) * 2 + core


def move(a, x=0, y=0, z=0, ways=(1, -1)):
    pairs = []
    for px in range(NX):
        for pz in range(NZ):
            for py in range(NY):
                for core, way in enumerate(ways):
                    to = place(px + way * x, py + way * y, (pz + way * z) % NZ, core)
                    pairs.append((place(px, py, pz, core), to))
    return lax.ppermute(a, AXES, pairs)


def swap_cores(a):
    pairs = [(n, n ^ 1) for n in range(NX * NY * NZ * 2)]
    return lax.ppermute(a, AXES, pairs)


def together(*arrays):
    return lax.optimization_barrier(arrays)


def dot_nt(a, b):
    return lax.dot_general(a, b, (((1,), (1,)), ((), ())), preferred_element_type=F32)


def run_copies(pairs, sems):
    copies = [pltpu.make_async_copy(a, b, sems.at[n]) for n, (a, b) in enumerate(pairs)]
    for copy in copies:
        copy.start()
    for copy in copies:
        copy.wait()


def columns(ref, start, size):
    return ref.at[:, pl.ds(pl.multiple_of(start, HEAD), size)]


def load_kernel(coord_ref, w_ref, k_ref, v_ref, load_ref):
    core = coord_ref[CORE]
    half = w_ref.shape[1] // 4
    shard = w_ref.shape[0]
    for n in range(2):
        start = pl.multiple_of((2 * n + core) * half, HEAD)
        load_ref[:shard, n * half : (n + 1) * half] = w_ref[:, pl.ds(start, half)]
    load_ref[shard : shard + TOK, :] = k_ref[...]
    load_ref[shard + TOK :, :] = v_ref[...]


def pick_load(coords, w, k, v):
    return pl.pallas_call(
        load_kernel,
        out_shape=jax.ShapeDtypeStruct((w.shape[0] + 2 * TOK, w.shape[1] // 2), BF),
        in_specs=[SMEM, VMEM, VMEM, VMEM],
        out_specs=VMEM,
        name="pick_load",
    )(coords, w, k, v)


def part_kernel(away, coord_ref, load_ref, hidden_ref, unit_ref, *part_refs):
    first = load_ref.shape[0] - 2 * TOK
    for n in range(2):
        unit_ref[n] = load_ref[first + n * TOK : first + (n + 1) * TOK, :]
    part = hidden_ref.shape[1] // NX
    for dx, ref in zip(away, part_refs):
        start = pl.multiple_of(lax.rem(coord_ref[X] + dx, NX) * part, HEAD)
        ref[...] = hidden_ref[:, pl.ds(start, part)]


def pick_parts(coords, load, hidden, away):
    part = jax.ShapeDtypeStruct((TOK, hidden.shape[1] // NX), BF)
    return pl.pallas_call(
        functools.partial(part_kernel, away),
        out_shape=(jax.ShapeDtypeStruct((2, TOK, load.shape[1]), BF),) + (part,) * len(away),
        in_specs=[SMEM, VMEM, VMEM],
        out_specs=(VMEM,) * (1 + len(away)),
        cost_estimate=pl.CostEstimate(flops=10**11, bytes_accessed=1000, transcendentals=0),
        name="pick_parts",
    )(coords, load, hidden)


def project_kernel(coord_ref, hidden_ref, *refs):
    peers, refs = refs[: NX - 1], refs[NX - 1 :]
    bundles, refs = refs[:4], refs[4:]
    own_ref, backs, (h_buf, w_buf, sems) = refs[0], refs[1:NX], refs[NX:]
    core, x, zl = coord_ref[CORE], coord_ref[X], coord_ref[ZL]
    part = h_buf.shape[1]
    pairs = [(columns(hidden_ref, x * part, part), h_buf.at[pl.ds(0, TOK)])]
    for n, ref in enumerate(peers):
        pairs.append((ref, h_buf.at[pl.ds((n + 1) * TOK, TOK)]))
    shard = part // NZL
    for ref, offsets, swapped in zip(bundles, (FIRST, SECOND) * 2, (0, 0, 1, 1)):
        from_core = 1 - core if swapped else core
        way = 1 - 2 * from_core
        for n, dz in enumerate(offsets):
            start = pl.multiple_of(lax.rem(zl - way * dz + NZL, NZL) * shard, 16)
            pairs.append((ref.at[pl.ds(n * shard, shard)], w_buf.at[from_core, pl.ds(start, shard)]))
    run_copies(pairs, sems)
    half = w_buf.shape[2] // 2
    keys = 2 * half
    for side in range(2):
        product = jnp.dot(h_buf[...], w_buf[side], preferred_element_type=F32)
        k, v = product[:, :half], product[:, half:]
        own_ref[:, side * half : (side + 1) * half] = k[:TOK]
        own_ref[:, keys + side * half : keys + (side + 1) * half] = v[:TOK]
        for n, ref in enumerate(backs):
            rows = slice((n + 1) * TOK, (n + 2) * TOK)
            high = k[rows].astype(BF)
            low = (k[rows] - high.astype(F32)).astype(BF)
            for i, value in enumerate((high, low, v[rows].astype(BF))):
                ref[:, i * keys + side * half : i * keys + (side + 1) * half] = value


def project(coords, hidden, peers, bundles):
    part = peers[0].shape[1]
    width = bundles[0].shape[1]
    back = jax.ShapeDtypeStruct((TOK, 3 * width), BF)
    return pl.pallas_call(
        project_kernel,
        out_shape=(jax.ShapeDtypeStruct((TOK, 2 * width), F32),) + (back,) * (NX - 1),
        in_specs=[SMEM] + [HBM] * (1 + len(peers) + len(bundles)),
        out_specs=(VMEM,) * NX,
        scratch_shapes=[
            pltpu.VMEM((NX * TOK, part), BF),
            pltpu.VMEM((2, part, width), BF),
            pltpu.SemaphoreType.DMA((NX + 2 * NZL,)),
        ],
        cost_estimate=pl.CostEstimate(flops=10**11, bytes_accessed=1000, transcendentals=0),
        name="project",
    )(coords, hidden, *peers, *bundles)


def pack_kernel(*refs):
    at = 0
    for ref in refs[:-1]:
        refs[-1][at : at + ref.shape[0]] = ref[...]
        at += ref.shape[0]


def pack(blocks, rank):
    return pl.pallas_call(
        pack_kernel,
        out_shape=jax.ShapeDtypeStruct((sum(a.shape[0] for a in blocks), *blocks[0].shape[1:]), BF),
        in_specs=[VMEM] * len(blocks),
        out_specs=VMEM,
        compiler_params=pltpu.CompilerParams(vmem_limit_bytes=SMALL_LIMIT),
        cost_estimate=pl.CostEstimate(flops=rank, bytes_accessed=1000, transcendentals=0),
        name="pack",
    )(*blocks)


def seen_tokens(mask_ref, fork_ref, block):
    count = jnp.clip(fork_ref[0] + 1 - block * TOK, 0, TOK)
    return jnp.where(mask_ref[0, block] == 1, count, 0)


def attention_kernel(stage, together_heads, coord_ref, mask_ref, fork_ref, q_ref, *refs):
    segment, carried = stage == 2, stage > 0
    if segment:
        (cos_ref, sin_ref, gain_ref, own_ref), refs = refs[:4], refs[4:]
        backs, refs = refs[: NX - 1], refs[NX - 1 :]
    elif stage == 0:
        blocks, refs = [*(refs[0].at[n] for n in range(NY)), *refs[1 : NY + 1]], refs[NY + 1 :]
    else:
        blocks, refs = [refs[0].at[n] for n in range(2 * NY)], refs[1:]
    if carried:
        (acc_in, top_in, total_in), refs = refs[:3], refs[3:]
    if segment:
        out_ref, refs = refs[0], refs[1:]
    else:
        (acc_ref, top_ref, total_ref), refs = refs[:3], refs[3:]
    k_buf, v_buf = refs
    groups = k_buf.shape[0]
    heads = q_ref.shape[1] // HEAD
    per_group = heads // groups

    def lanes_of(h):
        return slice(h * HEAD, (h + 1) * HEAD)

    for g in range(groups):
        v_buf[g, :, HEAD:] = jnp.ones((k_buf.shape[1], HEAD), BF)
        if segment:
            k, v = own_ref[:, lanes_of(g)], own_ref[:, lanes_of(groups + g)]
            for ref in backs:
                high, low = ref[:, lanes_of(g)], ref[:, lanes_of(groups + g)]
                k = k + (high.astype(F32) + low.astype(F32))
                v = v + ref[:, lanes_of(2 * groups + g)].astype(F32)
            k = k * lax.rsqrt(jnp.mean(k * k, axis=1, keepdims=True) + EPS) * gain_ref[...]
            k = k * cos_ref[...] + pltpu.roll(k, HEAD // 2, 1) * sin_ref[...]
            k_buf[g] = k.astype(BF)
            v_buf[g, :, :HEAD] = v.astype(BF)
        else:
            for i, ref in enumerate(blocks):
                rows = slice(i * TOK, (i + 1) * TOK)
                k_buf[g, rows, :] = ref[0, :, lanes_of(g)]
                v_buf[g, rows, :HEAD] = ref[1, :, lanes_of(g)]
    if segment:
        row = lax.broadcasted_iota(jnp.int32, (TOK, TOK), 0)
        column = lax.broadcasted_iota(jnp.int32, (TOK, TOK), 1)
        bias = jnp.where(row >= column, 0.0, FLOOR)
        bias = jnp.concatenate([bias] * together_heads, axis=0)
    else:
        core, y, zh = coord_ref[CORE], coord_ref[Y], coord_ref[ZH]
        from_core = core if stage == 0 else 1 - core
        lane = lax.broadcasted_iota(jnp.int32, (1, TOK), 1)
        bias = []
        for side in (zh, 1 - zh):
            for away in ROUND_Y:
                block = lax.rem(y - away + NY, NY) * 4 + side * 2 + from_core
                bias.append(jnp.where(lane < seen_tokens(mask_ref, fork_ref, block), 0.0, FLOOR))
        bias = jnp.concatenate(bias, axis=1)
    units = [range(h, h + together_heads) for h in range(0, heads, together_heads)]

    def score(unit):
        q = jnp.concatenate([q_ref[:, lanes_of(h)] for h in unit], axis=0)
        return dot_nt(q, k_buf[unit[0] // per_group])

    ahead = score(units[0])
    for n, unit in enumerate(units):
        scores = ahead + bias
        if n + 1 < len(units):
            ahead = score(units[n + 1])
        top = jnp.max(scores, axis=1, keepdims=True)
        if carried:
            old = jnp.concatenate([top_in[:, lanes_of(h)] for h in unit], axis=0)
            wide = jnp.maximum(old, top)
            factor = jnp.exp2((old - wide) * EXP_SCALE)
            top = jnp.concatenate([wide] * (scores.shape[1] // HEAD), axis=1)
        else:
            wide = jnp.broadcast_to(top, (top.shape[0], HEAD))
        weights = jnp.exp2((scores - top) * EXP_SCALE).astype(BF)
        summed = jnp.dot(weights, v_buf[unit[0] // per_group], preferred_element_type=F32)
        for i, h in enumerate(unit):
            rows = slice(i * TOK, (i + 1) * TOK)
            value, total = summed[rows, :HEAD], summed[rows, HEAD:]
            if carried:
                value = value + acc_in[:, lanes_of(h)] * factor[rows]
                total = total + total_in[:, lanes_of(h)] * factor[rows]
            if segment:
                out_ref[:, lanes_of(h)] = (value / total).astype(BF)
            else:
                acc_ref[:, lanes_of(h)] = value
                top_ref[:, lanes_of(h)] = wide[rows]
                total_ref[:, lanes_of(h)] = total


def attention(stage, coords, mask, fork, queries, groups, operands):
    width = queries.shape[1]
    heads = width // HEAD
    length = TOK if stage == 2 else 2 * NY * TOK
    if stage == 2:
        out_shape = jax.ShapeDtypeStruct((TOK, width), BF)
    else:
        out_shape = (jax.ShapeDtypeStruct((TOK, width), F32),) * 3
    return pl.pallas_call(
        functools.partial(attention_kernel, stage, 4 if stage == 2 else 2),
        out_shape=out_shape,
        in_specs=[SMEM] * 3 + [VMEM] * (1 + len(operands)),
        out_specs=VMEM if stage == 2 else (VMEM,) * 3,
        scratch_shapes=[
            pltpu.VMEM((groups, length, HEAD), BF),
            pltpu.VMEM((groups, length, 2 * HEAD), BF),
        ],
        compiler_params=pltpu.CompilerParams(vmem_limit_bytes=VMEM_LIMIT),
        cost_estimate=pl.CostEstimate(flops=10**9, bytes_accessed=1000, transcendentals=0),
        name=("own_blocks", "other_blocks", "segment_block")[stage],
    )(coords, mask, fork, queries, *operands)


def on_device(
    hidden,
    queries,
    key_value_weight,
    k_gain,
    cached_ancestor_keys,
    cached_ancestor_values,
    ancestor_mask,
    fork_offset,
):
    dp, leaf = lax.axis_index("dp"), lax.axis_index("leaf")
    coords = jnp.stack([leaf % 2, leaf // 4, (leaf // 2) % 2, dp // NZL, dp % NZL]).astype(jnp.int32)
    groups = cached_ancestor_keys.shape[3] // HEAD
    keys, values = cached_ancestor_keys[0, 0], cached_ancestor_values[0, 0]
    load = pick_load(coords, key_value_weight, keys, values)
    unit, *sent = pick_parts(coords, load, hidden[0], (1,))

    block_start = jnp.arange(ancestor_mask.shape[1], dtype=jnp.int32) * TOK
    seen = jnp.clip(fork_offset[:, None] + 1 - block_start[None, :], 0, TOK)
    start = jnp.sum(jnp.where(ancestor_mask == 1, seen, 0))
    positions = (start + jnp.arange(TOK, dtype=jnp.int32)).astype(F32)
    freq = THETA ** (-jnp.arange(HEAD // 2, dtype=F32) * 2.0 / HEAD)
    angle = positions[:, None] * freq
    cosine, sine = jnp.cos(angle), jnp.sin(angle)
    cosine = jnp.concatenate([cosine, cosine], axis=-1)
    sine = jnp.concatenate([-sine, sine], axis=-1)

    def direct(a, **by):
        return move(a, ways=(1, 1), **by)

    def to_y_peers(a):
        return [direct(a, y=n) for n in ROUND_Y[1:]]

    shard = key_value_weight.shape[0]
    got = move(load, z=4)
    fours = jnp.concatenate([load[:shard], got[:shard]], axis=0)
    fours, far, part_one, *near = together(
        fours, got[shard:].reshape(unit.shape), direct(sent[0], x=1), *to_y_peers(unit)
    )
    _, *sent = pick_parts(coords, got, hidden[0], (2, 3))
    far, two, part_two, part_three, cosine, sine = together(
        move(far, z=4), move(fours, z=2), direct(sent[0], x=2), direct(sent[1], x=3), cosine, sine
    )
    first = jnp.concatenate([fours, two], axis=0)
    second, other_first = together(move(first, z=1), swap_cores(first))
    other_second = swap_cores(second)
    peers = [part_one, part_two, part_three]
    partial, *backs = project(coords, hidden[0], peers, [first, second, other_first, other_second])
    backs = [direct(backs[n - 1], x=-n) for n in (2, 3, 1)]
    near = pack([unit, *near], 10**13)
    far = [far, *to_y_peers(far)]
    other = swap_cores(pack([near, *far], 10**6)).reshape(2 * NY, *unit.shape)
    blocks = [near.reshape(NY, *unit.shape), *far]

    given = (coords, ancestor_mask, fork_offset, queries[0], groups)
    state = attention(0, *given, blocks)
    state = attention(1, *given, [other, *state])
    result = attention(2, *given, [cosine, sine, k_gain[None, :], partial, *backs, *state])
    return result[None]


def solution(mesh):
    in_specs = (
        P(("dp", "leaf"), None, None),
        P(("dp", "leaf"), None, None),
        P("dp", None),
        P(),
        P("dp", "leaf", None, None),
        P("dp", "leaf", None, None),
        P(("dp", "leaf"), None),
        P(("dp", "leaf")),
    )
    out_specs = P(("dp", "leaf"), None, None)
    return jax.shard_map(
        on_device, mesh=mesh, in_specs=in_specs, out_specs=out_specs, check_vma=False
    )
```

```python
import functools
import math

import jax
import jax.numpy as jnp
from jax import lax
from jax.experimental import pallas as pl
from jax.experimental.pallas import tpu as pltpu
from jax.sharding import PartitionSpec as P

EPS = 1e-06
THETA = 1000000.0
HEAD = 128
TOK = 128
FLOOR = -1e30
EXP_SCALE = HEAD ** (-0.5) * math.log2(math.e)
AXES = ("dp", "leaf")
NX, NZL, NY, NZH = 4, 8, 4, 2
NZ = NZL * NZH
BF = jnp.bfloat16
F32 = jnp.float32
VMEM = pl.BlockSpec(memory_space=pltpu.VMEM)
SMEM = pl.BlockSpec(memory_space=pltpu.SMEM)
HBM = pl.BlockSpec(memory_space=pltpu.HBM)
VMEM_LIMIT = 36 * 2**20
SMALL_LIMIT = 24 * 2**20
CORE, Y, ZH, X, ZL = range(5)
FIRST, SECOND = (0, 4, 2, 6), (1, 5, 3, 7)
ROUND_Y = (0, 2, 1, 3)


def place(x, y, z, core):
    return ((x % NX * NZL + z % NZL) * NY + y % NY) * 4 + (z // NZL % NZH) * 2 + core


def move(a, x=0, y=0, z=0, ways=(1, -1)):
    pairs = []
    for px in range(NX):
        for pz in range(NZ):
            for py in range(NY):
                for core, way in enumerate(ways):
                    to = place(px + way * x, py + way * y, (pz + way * z) % NZ, core)
                    pairs.append((place(px, py, pz, core), to))
    return lax.ppermute(a, AXES, pairs)


def swap_cores(a):
    pairs = [(n, n ^ 1) for n in range(NX * NY * NZ * 2)]
    return lax.ppermute(a, AXES, pairs)


def together(*arrays):
    return lax.optimization_barrier(arrays)


def dot_nt(a, b):
    return lax.dot_general(a, b, (((1,), (1,)), ((), ())), preferred_element_type=F32)


def run_copies(pairs, sems):
    copies = [pltpu.make_async_copy(a, b, sems.at[n]) for n, (a, b) in enumerate(pairs)]
    for copy in copies:
        copy.start()
    for copy in copies:
        copy.wait()


def columns(ref, start, size):
    return ref.at[:, pl.ds(pl.multiple_of(start, HEAD), size)]


def load_kernel(coord_ref, w_ref, k_ref, v_ref, load_ref):
    core = coord_ref[CORE]
    half = w_ref.shape[1] // 4
    shard = w_ref.shape[0]
    for n in range(2):
        start = pl.multiple_of((2 * n + core) * half, HEAD)
        load_ref[:shard, n * half : (n + 1) * half] = w_ref[:, pl.ds(start, half)]
    load_ref[shard : shard + TOK, :] = k_ref[...]
    load_ref[shard + TOK :, :] = v_ref[...]


def pick_load(coords, w, k, v):
    return pl.pallas_call(
        load_kernel,
        out_shape=jax.ShapeDtypeStruct((w.shape[0] + 2 * TOK, w.shape[1] // 2), BF),
        in_specs=[SMEM, VMEM, VMEM, VMEM],
        out_specs=VMEM,
        name="pick_load",
    )(coords, w, k, v)


def part_kernel(away, coord_ref, load_ref, hidden_ref, unit_ref, *part_refs):
    first = load_ref.shape[0] - 2 * TOK
    for n in range(2):
        unit_ref[n] = load_ref[first + n * TOK : first + (n + 1) * TOK, :]
    part = hidden_ref.shape[1] // NX
    for dx, ref in zip(away, part_refs):
        start = pl.multiple_of(lax.rem(coord_ref[X] + dx, NX) * part, HEAD)
        ref[...] = hidden_ref[:, pl.ds(start, part)]


def pick_parts(coords, load, hidden, away):
    part = jax.ShapeDtypeStruct((TOK, hidden.shape[1] // NX), BF)
    return pl.pallas_call(
        functools.partial(part_kernel, away),
        out_shape=(jax.ShapeDtypeStruct((2, TOK, load.shape[1]), BF),) + (part,) * len(away),
        in_specs=[SMEM, VMEM, VMEM],
        out_specs=(VMEM,) * (1 + len(away)),
        cost_estimate=pl.CostEstimate(flops=10**11, bytes_accessed=1000, transcendentals=0),
        name="pick_parts",
    )(coords, load, hidden)


def project_kernel(coord_ref, hidden_ref, *refs):
    peers, refs = refs[: NX - 1], refs[NX - 1 :]
    bundles, refs = refs[:4], refs[4:]
    own_ref, backs, (h_buf, w_buf, sems) = refs[0], refs[1:NX], refs[NX:]
    core, x, zl = coord_ref[CORE], coord_ref[X], coord_ref[ZL]
    part = h_buf.shape[1]
    pairs = [(columns(hidden_ref, x * part, part), h_buf.at[pl.ds(0, TOK)])]
    for n, ref in enumerate(peers):
        pairs.append((ref, h_buf.at[pl.ds((n + 1) * TOK, TOK)]))
    shard = part // NZL
    for ref, offsets, swapped in zip(bundles, (FIRST, SECOND) * 2, (0, 0, 1, 1)):
        from_core = 1 - core if swapped else core
        way = 1 - 2 * from_core
        for n, dz in enumerate(offsets):
            start = pl.multiple_of(lax.rem(zl - way * dz + NZL, NZL) * shard, 16)
            pairs.append((ref.at[pl.ds(n * shard, shard)], w_buf.at[from_core, pl.ds(start, shard)]))
    run_copies(pairs, sems)
    half = w_buf.shape[2] // 2
    keys = 2 * half
    for side in range(2):
        product = jnp.dot(h_buf[...], w_buf[side], preferred_element_type=F32)
        k, v = product[:, :half], product[:, half:]
        own_ref[:, side * half : (side + 1) * half] = k[:TOK]
        own_ref[:, keys + side * half : keys + (side + 1) * half] = v[:TOK]
        for n, ref in enumerate(backs):
            rows = slice((n + 1) * TOK, (n + 2) * TOK)
            high = k[rows].astype(BF)
            low = (k[rows] - high.astype(F32)).astype(BF)
            for i, value in enumerate((high, low, v[rows].astype(BF))):
                ref[:, i * keys + side * half : i * keys + (side + 1) * half] = value


def project(coords, hidden, peers, bundles):
    part = peers[0].shape[1]
    width = bundles[0].shape[1]
    back = jax.ShapeDtypeStruct((TOK, 3 * width), BF)
    return pl.pallas_call(
        project_kernel,
        out_shape=(jax.ShapeDtypeStruct((TOK, 2 * width), F32),) + (back,) * (NX - 1),
        in_specs=[SMEM] + [HBM] * (1 + len(peers) + len(bundles)),
        out_specs=(VMEM,) * NX,
        scratch_shapes=[
            pltpu.VMEM((NX * TOK, part), BF),
            pltpu.VMEM((2, part, width), BF),
            pltpu.SemaphoreType.DMA((NX + 2 * NZL,)),
        ],
        cost_estimate=pl.CostEstimate(flops=10**11, bytes_accessed=1000, transcendentals=0),
        name="project",
    )(coords, hidden, *peers, *bundles)


def pack_kernel(*refs):
    at = 0
    for ref in refs[:-1]:
        refs[-1][at : at + ref.shape[0]] = ref[...]
        at += ref.shape[0]


def pack(blocks, rank):
    return pl.pallas_call(
        pack_kernel,
        out_shape=jax.ShapeDtypeStruct((sum(a.shape[0] for a in blocks), *blocks[0].shape[1:]), BF),
        in_specs=[VMEM] * len(blocks),
        out_specs=VMEM,
        compiler_params=pltpu.CompilerParams(vmem_limit_bytes=SMALL_LIMIT),
        cost_estimate=pl.CostEstimate(flops=rank, bytes_accessed=1000, transcendentals=0),
        name="pack",
    )(*blocks)


def seen_tokens(mask_ref, fork_ref, block):
    count = jnp.clip(fork_ref[0] + 1 - block * TOK, 0, TOK)
    return jnp.where(mask_ref[0, block] == 1, count, 0)


def attention_kernel(stage, together_heads, coord_ref, mask_ref, fork_ref, q_ref, *refs):
    segment, carried = stage == 2, stage > 0
    if segment:
        (cos_ref, sin_ref, gain_ref, own_ref), refs = refs[:4], refs[4:]
        backs, refs = refs[: NX - 1], refs[NX - 1 :]
    elif stage == 0:
        blocks, refs = [*(refs[0].at[n] for n in range(NY)), *refs[1 : NY + 1]], refs[NY + 1 :]
    else:
        blocks, refs = [refs[0].at[n] for n in range(2 * NY)], refs[1:]
    if carried:
        (acc_in, top_in, total_in), refs = refs[:3], refs[3:]
    if segment:
        out_ref, refs = refs[0], refs[1:]
    else:
        (acc_ref, top_ref, total_ref), refs = refs[:3], refs[3:]
    k_buf, v_buf = refs
    groups = k_buf.shape[0]
    heads = q_ref.shape[1] // HEAD
    per_group = heads // groups

    def lanes_of(h):
        return slice(h * HEAD, (h + 1) * HEAD)

    for g in range(groups):
        v_buf[g, :, HEAD:] = jnp.ones((k_buf.shape[1], HEAD), BF)
        if segment:
            k, v = own_ref[:, lanes_of(g)], own_ref[:, lanes_of(groups + g)]
            for ref in backs:
                high, low = ref[:, lanes_of(g)], ref[:, lanes_of(groups + g)]
                k = k + (high.astype(F32) + low.astype(F32))
                v = v + ref[:, lanes_of(2 * groups + g)].astype(F32)
            k = k * lax.rsqrt(jnp.mean(k * k, axis=1, keepdims=True) + EPS) * gain_ref[...]
            k = k * cos_ref[...] + pltpu.roll(k, HEAD // 2, 1) * sin_ref[...]
            k_buf[g] = k.astype(BF)
            v_buf[g, :, :HEAD] = v.astype(BF)
        else:
            for i, ref in enumerate(blocks):
                rows = slice(i * TOK, (i + 1) * TOK)
                k_buf[g, rows, :] = ref[0, :, lanes_of(g)]
                v_buf[g, rows, :HEAD] = ref[1, :, lanes_of(g)]
    if segment:
        row = lax.broadcasted_iota(jnp.int32, (TOK, TOK), 0)
        column = lax.broadcasted_iota(jnp.int32, (TOK, TOK), 1)
        bias = jnp.where(row >= column, 0.0, FLOOR)
        bias = jnp.concatenate([bias] * together_heads, axis=0)
    else:
        core, y, zh = coord_ref[CORE], coord_ref[Y], coord_ref[ZH]
        from_core = core if stage == 0 else 1 - core
        lane = lax.broadcasted_iota(jnp.int32, (1, TOK), 1)
        bias = []
        for side in (zh, 1 - zh):
            for away in ROUND_Y:
                block = lax.rem(y - away + NY, NY) * 4 + side * 2 + from_core
                bias.append(jnp.where(lane < seen_tokens(mask_ref, fork_ref, block), 0.0, FLOOR))
        bias = jnp.concatenate(bias, axis=1)
    units = [range(h, h + together_heads) for h in range(0, heads, together_heads)]

    def score(unit):
        q = jnp.concatenate([q_ref[:, lanes_of(h)] for h in unit], axis=0)
        return dot_nt(q, k_buf[unit[0] // per_group])

    ahead = score(units[0])
    for n, unit in enumerate(units):
        scores = ahead + bias
        if n + 1 < len(units):
            ahead = score(units[n + 1])
        top = jnp.max(scores, axis=1, keepdims=True)
        if carried:
            old = jnp.concatenate([top_in[:, lanes_of(h)] for h in unit], axis=0)
            wide = jnp.maximum(old, top)
            factor = jnp.exp2((old - wide) * EXP_SCALE)
            top = jnp.concatenate([wide] * (scores.shape[1] // HEAD), axis=1)
        else:
            wide = jnp.broadcast_to(top, (top.shape[0], HEAD))
        weights = jnp.exp2((scores - top) * EXP_SCALE).astype(BF)
        summed = jnp.dot(weights, v_buf[unit[0] // per_group], preferred_element_type=F32)
        for i, h in enumerate(unit):
            rows = slice(i * TOK, (i + 1) * TOK)
            value, total = summed[rows, :HEAD], summed[rows, HEAD:]
            if carried:
                value = value + acc_in[:, lanes_of(h)] * factor[rows]
                total = total + total_in[:, lanes_of(h)] * factor[rows]
            if segment:
                out_ref[:, lanes_of(h)] = (value / total).astype(BF)
            else:
                acc_ref[:, lanes_of(h)] = value
                top_ref[:, lanes_of(h)] = wide[rows]
                total_ref[:, lanes_of(h)] = total


def attention(stage, coords, mask, fork, queries, groups, operands):
    width = queries.shape[1]
    heads = width // HEAD
    length = TOK if stage == 2 else 2 * NY * TOK
    if stage == 2:
        out_shape = jax.ShapeDtypeStruct((TOK, width), BF)
    else:
        out_shape = (jax.ShapeDtypeStruct((TOK, width), F32),) * 3
    return pl.pallas_call(
        functools.partial(attention_kernel, stage, 4 if stage == 2 else 2),
        out_shape=out_shape,
        in_specs=[SMEM] * 3 + [VMEM] * (1 + len(operands)),
        out_specs=VMEM if stage == 2 else (VMEM,) * 3,
        scratch_shapes=[
            pltpu.VMEM((groups, length, HEAD), BF),
            pltpu.VMEM((groups, length, 2 * HEAD), BF),
        ],
        compiler_params=pltpu.CompilerParams(vmem_limit_bytes=VMEM_LIMIT),
        cost_estimate=pl.CostEstimate(flops=10**9, bytes_accessed=1000, transcendentals=0),
        name=("own_blocks", "other_blocks", "segment_block")[stage],
    )(coords, mask, fork, queries, *operands)


def on_device(
    hidden,
    queries,
    key_value_weight,
    k_gain,
    cached_ancestor_keys,
    cached_ancestor_values,
    ancestor_mask,
    fork_offset,
):
    dp, leaf = lax.axis_index("dp"), lax.axis_index("leaf")
    coords = jnp.stack([leaf % 2, leaf // 4, (leaf // 2) % 2, dp // NZL, dp % NZL]).astype(jnp.int32)
    groups = cached_ancestor_keys.shape[3] // HEAD
    keys, values = cached_ancestor_keys[0, 0], cached_ancestor_values[0, 0]
    load = pick_load(coords, key_value_weight, keys, values)
    unit, *_ = pick_parts(coords, load, hidden[0], ())

    block_start = jnp.arange(ancestor_mask.shape[1], dtype=jnp.int32) * TOK
    seen = jnp.clip(fork_offset[:, None] + 1 - block_start[None, :], 0, TOK)
    start = jnp.sum(jnp.where(ancestor_mask == 1, seen, 0))
    positions = (start + jnp.arange(TOK, dtype=jnp.int32)).astype(F32)
    freq = THETA ** (-jnp.arange(HEAD // 2, dtype=F32) * 2.0 / HEAD)
    angle = positions[:, None] * freq
    cosine, sine = jnp.cos(angle), jnp.sin(angle)
    cosine = jnp.concatenate([cosine, cosine], axis=-1)
    sine = jnp.concatenate([-sine, sine], axis=-1)

    def direct(a, **by):
        return move(a, ways=(1, 1), **by)

    def to_y_peers(a):
        return [direct(a, y=n) for n in ROUND_Y[1:]]

    shard = key_value_weight.shape[0]
    got = move(load, z=4)
    fours = jnp.concatenate([load[:shard], got[:shard]], axis=0)
    fours, far, *near = together(fours, got[shard:].reshape(unit.shape), *to_y_peers(unit))
    _, *sent = pick_parts(coords, got, hidden[0], (1, 2, 3))
    far, two, part_two, part_one, part_three, cosine, sine = together(
        move(far, z=4), move(fours, z=2), *(direct(sent[n - 1], x=n) for n in (2, 1, 3)), cosine, sine
    )
    first = jnp.concatenate([fours, two], axis=0)
    second, other_first = together(move(first, z=1), swap_cores(first))
    other_second = swap_cores(second)
    peers = [part_one, part_two, part_three]
    partial, *backs = project(coords, hidden[0], peers, [first, second, other_first, other_second])
    backs = [direct(backs[n - 1], x=-n) for n in (2, 3, 1)]
    near = pack([unit, *near], 10**13)
    far = [far, *to_y_peers(far)]
    other = swap_cores(pack([near, *far], 10**6)).reshape(2 * NY, *unit.shape)
    blocks = [near.reshape(NY, *unit.shape), *far]

    given = (coords, ancestor_mask, fork_offset, queries[0], groups)
    state = attention(0, *given, blocks)
    state = attention(1, *given, [other, *state])
    result = attention(2, *given, [cosine, sine, k_gain[None, :], partial, *backs, *state])
    return result[None]


def solution(mesh):
    in_specs = (
        P(("dp", "leaf"), None, None),
        P(("dp", "leaf"), None, None),
        P("dp", None),
        P(),
        P("dp", "leaf", None, None),
        P("dp", "leaf", None, None),
        P(("dp", "leaf"), None),
        P(("dp", "leaf")),
    )
    out_specs = P(("dp", "leaf"), None, None)
    return jax.shard_map(
        on_device, mesh=mesh, in_specs=in_specs, out_specs=out_specs, check_vma=False
    )
```

```python
import functools
import math

import jax
import jax.numpy as jnp
from jax import lax
from jax.experimental import pallas as pl
from jax.experimental.pallas import tpu as pltpu
from jax.sharding import PartitionSpec as P

EPS = 1e-06
THETA = 1000000.0
HEAD = 128
TOK = 128
FLOOR = -1e30
EXP_SCALE = HEAD ** (-0.5) * math.log2(math.e)
AXES = ("dp", "leaf")
NX, NZL, NY, NZH = 4, 8, 4, 2
NZ = NZL * NZH
BF = jnp.bfloat16
F32 = jnp.float32
VMEM = pl.BlockSpec(memory_space=pltpu.VMEM)
SMEM = pl.BlockSpec(memory_space=pltpu.SMEM)
HBM = pl.BlockSpec(memory_space=pltpu.HBM)
VMEM_LIMIT = 36 * 2**20
SMALL_LIMIT = 24 * 2**20
CORE, Y, ZH, X, ZL = range(5)
FIRST, SECOND = (0, 4, 2, 6), (1, 5, 3, 7)
ROUND_Y = (0, 2, 1, 3)


def place(x, y, z, core):
    return ((x % NX * NZL + z % NZL) * NY + y % NY) * 4 + (z // NZL % NZH) * 2 + core


def move(a, x=0, y=0, z=0, ways=(1, -1)):
    pairs = []
    for px in range(NX):
        for pz in range(NZ):
            for py in range(NY):
                for core, way in enumerate(ways):
                    to = place(px + way * x, py + way * y, (pz + way * z) % NZ, core)
                    pairs.append((place(px, py, pz, core), to))
    return lax.ppermute(a, AXES, pairs)


def swap_cores(a):
    pairs = [(n, n ^ 1) for n in range(NX * NY * NZ * 2)]
    return lax.ppermute(a, AXES, pairs)


def together(*arrays):
    return lax.optimization_barrier(arrays)


def dot_nt(a, b):
    return lax.dot_general(a, b, (((1,), (1,)), ((), ())), preferred_element_type=F32)


def run_copies(pairs, sems):
    copies = [pltpu.make_async_copy(a, b, sems.at[n]) for n, (a, b) in enumerate(pairs)]
    for copy in copies:
        copy.start()
    for copy in copies:
        copy.wait()


def columns(ref, start, size):
    return ref.at[:, pl.ds(pl.multiple_of(start, HEAD), size)]


def load_kernel(coord_ref, w_ref, k_ref, v_ref, load_ref):
    core = coord_ref[CORE]
    half = w_ref.shape[1] // 4
    shard = w_ref.shape[0]
    for n in range(2):
        start = pl.multiple_of((2 * n + core) * half, HEAD)
        load_ref[:shard, n * half : (n + 1) * half] = w_ref[:, pl.ds(start, half)]
    load_ref[shard : shard + TOK, :] = k_ref[...]
    load_ref[shard + TOK :, :] = v_ref[...]


def pick_load(coords, w, k, v):
    return pl.pallas_call(
        load_kernel,
        out_shape=jax.ShapeDtypeStruct((w.shape[0] + 2 * TOK, w.shape[1] // 2), BF),
        in_specs=[SMEM, VMEM, VMEM, VMEM],
        out_specs=VMEM,
        name="pick_load",
    )(coords, w, k, v)


def unit_kernel(load_ref, unit_ref):
    first = load_ref.shape[0] - 2 * TOK
    for n in range(2):
        unit_ref[n] = load_ref[first + n * TOK : first + (n + 1) * TOK, :]


def pick_unit(load):
    return pl.pallas_call(
        unit_kernel,
        out_shape=jax.ShapeDtypeStruct((2, TOK, load.shape[1]), BF),
        in_specs=[VMEM],
        out_specs=VMEM,
        cost_estimate=pl.CostEstimate(flops=10**11, bytes_accessed=1000, transcendentals=0),
        name="pick_unit",
    )(load)


def part_kernel(coord_ref, _, hidden_ref, *part_refs):
    part = hidden_ref.shape[1] // NX
    for n, ref in enumerate(part_refs):
        start = pl.multiple_of(lax.rem(coord_ref[X] + n + 1, NX) * part, HEAD)
        ref[...] = hidden_ref[:, pl.ds(start, part)]


def pick_parts(coords, before, hidden):
    part = jax.ShapeDtypeStruct((TOK, hidden.shape[1] // NX), BF)
    return pl.pallas_call(
        part_kernel,
        out_shape=(part,) * (NX - 1),
        in_specs=[SMEM, HBM, VMEM],
        out_specs=(VMEM,) * (NX - 1),
        cost_estimate=pl.CostEstimate(flops=10**11, bytes_accessed=1000, transcendentals=0),
        name="pick_parts",
    )(coords, before, hidden)


def project_kernel(coord_ref, hidden_ref, *refs):
    peers, refs = refs[: NX - 1], refs[NX - 1 :]
    bundles, refs = refs[:4], refs[4:]
    own_ref, backs, (h_buf, w_buf, sems) = refs[0], refs[1:NX], refs[NX:]
    core, x, zl = coord_ref[CORE], coord_ref[X], coord_ref[ZL]
    part = h_buf.shape[1]
    pairs = [(columns(hidden_ref, x * part, part), h_buf.at[pl.ds(0, TOK)])]
    for n, ref in enumerate(peers):
        pairs.append((ref, h_buf.at[pl.ds((n + 1) * TOK, TOK)]))
    shard = part // NZL
    for ref, offsets, swapped in zip(bundles, (FIRST, SECOND) * 2, (0, 0, 1, 1)):
        from_core = 1 - core if swapped else core
        way = 1 - 2 * from_core
        for n, dz in enumerate(offsets):
            start = pl.multiple_of(lax.rem(zl - way * dz + NZL, NZL) * shard, 16)
            pairs.append((ref.at[pl.ds(n * shard, shard)], w_buf.at[from_core, pl.ds(start, shard)]))
    run_copies(pairs, sems)
    half = w_buf.shape[2] // 2
    keys = 2 * half
    for side in range(2):
        product = jnp.dot(h_buf[...], w_buf[side], preferred_element_type=F32)
        k, v = product[:, :half], product[:, half:]
        own_ref[:, side * half : (side + 1) * half] = k[:TOK]
        own_ref[:, keys + side * half : keys + (side + 1) * half] = v[:TOK]
        for n, ref in enumerate(backs):
            rows = slice((n + 1) * TOK, (n + 2) * TOK)
            high = k[rows].astype(BF)
            low = (k[rows] - high.astype(F32)).astype(BF)
            for i, value in enumerate((high, low, v[rows].astype(BF))):
                ref[:, i * keys + side * half : i * keys + (side + 1) * half] = value


def project(coords, hidden, peers, bundles):
    part = peers[0].shape[1]
    width = bundles[0].shape[1]
    back = jax.ShapeDtypeStruct((TOK, 3 * width), BF)
    return pl.pallas_call(
        project_kernel,
        out_shape=(jax.ShapeDtypeStruct((TOK, 2 * width), F32),) + (back,) * (NX - 1),
        in_specs=[SMEM] + [HBM] * (1 + len(peers) + len(bundles)),
        out_specs=(VMEM,) * NX,
        scratch_shapes=[
            pltpu.VMEM((NX * TOK, part), BF),
            pltpu.VMEM((2, part, width), BF),
            pltpu.SemaphoreType.DMA((NX + 2 * NZL,)),
        ],
        cost_estimate=pl.CostEstimate(flops=10**11, bytes_accessed=1000, transcendentals=0),
        name="project",
    )(coords, hidden, *peers, *bundles)


def pack_kernel(*refs):
    at = 0
    for ref in refs[:-1]:
        refs[-1][at : at + ref.shape[0]] = ref[...]
        at += ref.shape[0]


def pack(blocks, rank):
    return pl.pallas_call(
        pack_kernel,
        out_shape=jax.ShapeDtypeStruct((sum(a.shape[0] for a in blocks), *blocks[0].shape[1:]), BF),
        in_specs=[VMEM] * len(blocks),
        out_specs=VMEM,
        compiler_params=pltpu.CompilerParams(vmem_limit_bytes=SMALL_LIMIT),
        cost_estimate=pl.CostEstimate(flops=rank, bytes_accessed=1000, transcendentals=0),
        name="pack",
    )(*blocks)


def seen_tokens(mask_ref, fork_ref, block):
    count = jnp.clip(fork_ref[0] + 1 - block * TOK, 0, TOK)
    return jnp.where(mask_ref[0, block] == 1, count, 0)


def attention_kernel(stage, together_heads, coord_ref, mask_ref, fork_ref, q_ref, *refs):
    segment, carried = stage == 2, stage > 0
    if segment:
        (cos_ref, sin_ref, gain_ref, own_ref), refs = refs[:4], refs[4:]
        backs, refs = refs[: NX - 1], refs[NX - 1 :]
    elif stage == 0:
        blocks, refs = [*(refs[0].at[n] for n in range(NY)), *refs[1 : NY + 1]], refs[NY + 1 :]
    else:
        blocks, refs = [refs[0].at[n] for n in range(2 * NY)], refs[1:]
    if carried:
        (acc_in, top_in, total_in), refs = refs[:3], refs[3:]
    if segment:
        out_ref, refs = refs[0], refs[1:]
    else:
        (acc_ref, top_ref, total_ref), refs = refs[:3], refs[3:]
    k_buf, v_buf = refs
    groups = k_buf.shape[0]
    heads = q_ref.shape[1] // HEAD
    per_group = heads // groups

    def lanes_of(h):
        return slice(h * HEAD, (h + 1) * HEAD)

    for g in range(groups):
        v_buf[g, :, HEAD:] = jnp.ones((k_buf.shape[1], HEAD), BF)
        if segment:
            k, v = own_ref[:, lanes_of(g)], own_ref[:, lanes_of(groups + g)]
            for ref in backs:
                high, low = ref[:, lanes_of(g)], ref[:, lanes_of(groups + g)]
                k = k + (high.astype(F32) + low.astype(F32))
                v = v + ref[:, lanes_of(2 * groups + g)].astype(F32)
            k = k * lax.rsqrt(jnp.mean(k * k, axis=1, keepdims=True) + EPS) * gain_ref[...]
            k = k * cos_ref[...] + pltpu.roll(k, HEAD // 2, 1) * sin_ref[...]
            k_buf[g] = k.astype(BF)
            v_buf[g, :, :HEAD] = v.astype(BF)
        else:
            for i, ref in enumerate(blocks):
                rows = slice(i * TOK, (i + 1) * TOK)
                k_buf[g, rows, :] = ref[0, :, lanes_of(g)]
                v_buf[g, rows, :HEAD] = ref[1, :, lanes_of(g)]
    if segment:
        row = lax.broadcasted_iota(jnp.int32, (TOK, TOK), 0)
        column = lax.broadcasted_iota(jnp.int32, (TOK, TOK), 1)
        bias = jnp.where(row >= column, 0.0, FLOOR)
        bias = jnp.concatenate([bias] * together_heads, axis=0)
    else:
        core, y, zh = coord_ref[CORE], coord_ref[Y], coord_ref[ZH]
        from_core = core if stage == 0 else 1 - core
        lane = lax.broadcasted_iota(jnp.int32, (1, TOK), 1)
        bias = []
        for side in (zh, 1 - zh):
            for away in ROUND_Y:
                block = lax.rem(y - away + NY, NY) * 4 + side * 2 + from_core
                bias.append(jnp.where(lane < seen_tokens(mask_ref, fork_ref, block), 0.0, FLOOR))
        bias = jnp.concatenate(bias, axis=1)
    units = [range(h, h + together_heads) for h in range(0, heads, together_heads)]

    def score(unit):
        q = jnp.concatenate([q_ref[:, lanes_of(h)] for h in unit], axis=0)
        return dot_nt(q, k_buf[unit[0] // per_group])

    ahead = score(units[0])
    for n, unit in enumerate(units):
        scores = ahead + bias
        if n + 1 < len(units):
            ahead = score(units[n + 1])
        top = jnp.max(scores, axis=1, keepdims=True)
        if carried:
            old = jnp.concatenate([top_in[:, lanes_of(h)] for h in unit], axis=0)
            wide = jnp.maximum(old, top)
            factor = jnp.exp2((old - wide) * EXP_SCALE)
            top = jnp.concatenate([wide] * (scores.shape[1] // HEAD), axis=1)
        else:
            wide = jnp.broadcast_to(top, (top.shape[0], HEAD))
        weights = jnp.exp2((scores - top) * EXP_SCALE).astype(BF)
        summed = jnp.dot(weights, v_buf[unit[0] // per_group], preferred_element_type=F32)
        for i, h in enumerate(unit):
            rows = slice(i * TOK, (i + 1) * TOK)
            value, total = summed[rows, :HEAD], summed[rows, HEAD:]
            if carried:
                value = value + acc_in[:, lanes_of(h)] * factor[rows]
                total = total + total_in[:, lanes_of(h)] * factor[rows]
            if segment:
                out_ref[:, lanes_of(h)] = (value / total).astype(BF)
            else:
                acc_ref[:, lanes_of(h)] = value
                top_ref[:, lanes_of(h)] = wide[rows]
                total_ref[:, lanes_of(h)] = total


def attention(stage, coords, mask, fork, queries, groups, operands):
    width = queries.shape[1]
    heads = width // HEAD
    length = TOK if stage == 2 else 2 * NY * TOK
    if stage == 2:
        out_shape = jax.ShapeDtypeStruct((TOK, width), BF)
    else:
        out_shape = (jax.ShapeDtypeStruct((TOK, width), F32),) * 3
    return pl.pallas_call(
        functools.partial(attention_kernel, stage, 4 if stage == 2 else 2),
        out_shape=out_shape,
        in_specs=[SMEM] * 3 + [VMEM] * (1 + len(operands)),
        out_specs=VMEM if stage == 2 else (VMEM,) * 3,
        scratch_shapes=[
            pltpu.VMEM((groups, length, HEAD), BF),
            pltpu.VMEM((groups, length, 2 * HEAD), BF),
        ],
        compiler_params=pltpu.CompilerParams(vmem_limit_bytes=VMEM_LIMIT),
        cost_estimate=pl.CostEstimate(flops=10**9, bytes_accessed=1000, transcendentals=0),
        name=("own_blocks", "other_blocks", "segment_block")[stage],
    )(coords, mask, fork, queries, *operands)


def on_device(
    hidden,
    queries,
    key_value_weight,
    k_gain,
    cached_ancestor_keys,
    cached_ancestor_values,
    ancestor_mask,
    fork_offset,
):
    dp, leaf = lax.axis_index("dp"), lax.axis_index("leaf")
    coords = jnp.stack([leaf % 2, leaf // 4, (leaf // 2) % 2, dp // NZL, dp % NZL]).astype(jnp.int32)
    groups = cached_ancestor_keys.shape[3] // HEAD
    keys, values = cached_ancestor_keys[0, 0], cached_ancestor_values[0, 0]
    load = pick_load(coords, key_value_weight, keys, values)
    unit = pick_unit(load)

    block_start = jnp.arange(ancestor_mask.shape[1], dtype=jnp.int32) * TOK
    seen = jnp.clip(fork_offset[:, None] + 1 - block_start[None, :], 0, TOK)
    start = jnp.sum(jnp.where(ancestor_mask == 1, seen, 0))
    positions = (start + jnp.arange(TOK, dtype=jnp.int32)).astype(F32)
    freq = THETA ** (-jnp.arange(HEAD // 2, dtype=F32) * 2.0 / HEAD)
    angle = positions[:, None] * freq
    cosine, sine = jnp.cos(angle), jnp.sin(angle)
    cosine = jnp.concatenate([cosine, cosine], axis=-1)
    sine = jnp.concatenate([-sine, sine], axis=-1)

    def direct(a, **by):
        return move(a, ways=(1, 1), **by)

    def to_y_peers(a):
        return [direct(a, y=n) for n in ROUND_Y[1:]]

    shard = key_value_weight.shape[0]
    got = move(load, z=4)
    fours = jnp.concatenate([load[:shard], got[:shard]], axis=0)
    fours, far, *near = together(fours, got[shard:].reshape(unit.shape), *to_y_peers(unit))
    sent = pick_parts(coords, got, hidden[0])
    far, two, part_two, part_three, cosine, sine = together(
        move(far, z=4), move(fours, z=2), direct(sent[1], x=2), direct(sent[2], x=3), cosine, sine
    )
    first = jnp.concatenate([fours, two], axis=0)
    second, other_first, part_one = together(
        move(first, z=1), swap_cores(first), direct(sent[0], x=1)
    )
    other_second = swap_cores(second)
    peers = [part_one, part_two, part_three]
    partial, *backs = project(coords, hidden[0], peers, [first, second, other_first, other_second])
    backs = [direct(backs[n - 1], x=-n) for n in (2, 3, 1)]
    near = pack([unit, *near], 10**13)
    far = [far, *to_y_peers(far)]
    other = swap_cores(pack([near, *far], 10**6)).reshape(2 * NY, *unit.shape)
    blocks = [near.reshape(NY, *unit.shape), *far]

    given = (coords, ancestor_mask, fork_offset, queries[0], groups)
    state = attention(0, *given, blocks)
    state = attention(1, *given, [other, *state])
    result = attention(2, *given, [cosine, sine, k_gain[None, :], partial, *backs, *state])
    return result[None]


def solution(mesh):
    in_specs = (
        P(("dp", "leaf"), None, None),
        P(("dp", "leaf"), None, None),
        P("dp", None),
        P(),
        P("dp", "leaf", None, None),
        P("dp", "leaf", None, None),
        P(("dp", "leaf"), None),
        P(("dp", "leaf")),
    )
    out_specs = P(("dp", "leaf"), None, None)
    return jax.shard_map(
        on_device, mesh=mesh, in_specs=in_specs, out_specs=out_specs, check_vma=False
    )
```

```python
import functools
import math

import jax
import jax.numpy as jnp
from jax import lax
from jax.experimental import pallas as pl
from jax.experimental.pallas import tpu as pltpu
from jax.sharding import PartitionSpec as P

EPS = 1e-06
THETA = 1000000.0
HEAD = 128
TOK = 128
FLOOR = -1e30
EXP_SCALE = HEAD ** (-0.5) * math.log2(math.e)
AXES = ("dp", "leaf")
NX, NZL, NY, NZH = 4, 8, 4, 2
NZ = NZL * NZH
BF = jnp.bfloat16
F32 = jnp.float32
VMEM = pl.BlockSpec(memory_space=pltpu.VMEM)
SMEM = pl.BlockSpec(memory_space=pltpu.SMEM)
HBM = pl.BlockSpec(memory_space=pltpu.HBM)
VMEM_LIMIT = 36 * 2**20
SMALL_LIMIT = 24 * 2**20
CORE, Y, ZH, X, ZL = range(5)
FIRST, SECOND = (0, 4, 2, 6), (1, 5, 3, 7)
ROUND_Y = (0, 2, 1, 3)


def place(x, y, z, core):
    return ((x % NX * NZL + z % NZL) * NY + y % NY) * 4 + (z // NZL % NZH) * 2 + core


def move(a, x=0, y=0, z=0, ways=(1, -1)):
    pairs = []
    for px in range(NX):
        for pz in range(NZ):
            for py in range(NY):
                for core, way in enumerate(ways):
                    to = place(px + way * x, py + way * y, (pz + way * z) % NZ, core)
                    pairs.append((place(px, py, pz, core), to))
    return lax.ppermute(a, AXES, pairs)


def swap_cores(a):
    pairs = [(n, n ^ 1) for n in range(NX * NY * NZ * 2)]
    return lax.ppermute(a, AXES, pairs)


def together(*arrays):
    return lax.optimization_barrier(arrays)


def dot_nt(a, b):
    return lax.dot_general(a, b, (((1,), (1,)), ((), ())), preferred_element_type=F32)


def run_copies(pairs, sems):
    copies = [pltpu.make_async_copy(a, b, sems.at[n]) for n, (a, b) in enumerate(pairs)]
    for copy in copies:
        copy.start()
    for copy in copies:
        copy.wait()


def columns(ref, start, size):
    return ref.at[:, pl.ds(pl.multiple_of(start, HEAD), size)]


def load_kernel(coord_ref, w_ref, k_ref, v_ref, load_ref):
    core = coord_ref[CORE]
    half = w_ref.shape[1] // 4
    shard = w_ref.shape[0]
    for n in range(2):
        start = pl.multiple_of((2 * n + core) * half, HEAD)
        load_ref[:shard, n * half : (n + 1) * half] = w_ref[:, pl.ds(start, half)]
    load_ref[shard : shard + TOK, :] = k_ref[...]
    load_ref[shard + TOK :, :] = v_ref[...]


def pick_load(coords, w, k, v):
    return pl.pallas_call(
        load_kernel,
        out_shape=jax.ShapeDtypeStruct((w.shape[0] + 2 * TOK, w.shape[1] // 2), BF),
        in_specs=[SMEM, VMEM, VMEM, VMEM],
        out_specs=VMEM,
        name="pick_load",
    )(coords, w, k, v)


def unit_kernel(load_ref, unit_ref):
    first = load_ref.shape[0] - 2 * TOK
    for n in range(2):
        unit_ref[n] = load_ref[first + n * TOK : first + (n + 1) * TOK, :]


def pick_unit(load):
    return pl.pallas_call(
        unit_kernel,
        out_shape=jax.ShapeDtypeStruct((2, TOK, load.shape[1]), BF),
        in_specs=[VMEM],
        out_specs=VMEM,
        cost_estimate=pl.CostEstimate(flops=10**11, bytes_accessed=1000, transcendentals=0),
        name="pick_unit",
    )(load)


def part_kernel(coord_ref, _, hidden_ref, *part_refs):
    part = hidden_ref.shape[1] // NX
    for n, ref in enumerate(part_refs):
        start = pl.multiple_of(lax.rem(coord_ref[X] + n + 1, NX) * part, HEAD)
        ref[...] = hidden_ref[:, pl.ds(start, part)]


def pick_parts(coords, before, hidden):
    part = jax.ShapeDtypeStruct((TOK, hidden.shape[1] // NX), BF)
    return pl.pallas_call(
        part_kernel,
        out_shape=(part,) * (NX - 1),
        in_specs=[SMEM, HBM, VMEM],
        out_specs=(VMEM,) * (NX - 1),
        cost_estimate=pl.CostEstimate(flops=10**11, bytes_accessed=1000, transcendentals=0),
        name="pick_parts",
    )(coords, before, hidden)


def project_kernel(coord_ref, hidden_ref, *refs):
    peers, refs = refs[: NX - 1], refs[NX - 1 :]
    bundles, refs = refs[:4], refs[4:]
    own_ref, backs, (h_buf, w_buf, sems) = refs[0], refs[1:NX], refs[NX:]
    core, x, zl = coord_ref[CORE], coord_ref[X], coord_ref[ZL]
    part = h_buf.shape[1]
    pairs = [(columns(hidden_ref, x * part, part), h_buf.at[pl.ds(0, TOK)])]
    for n, ref in enumerate(peers):
        pairs.append((ref, h_buf.at[pl.ds((n + 1) * TOK, TOK)]))
    shard = part // NZL
    for ref, offsets, swapped in zip(bundles, (FIRST, SECOND) * 2, (0, 0, 1, 1)):
        from_core = 1 - core if swapped else core
        way = 1 - 2 * from_core
        for n, dz in enumerate(offsets):
            start = pl.multiple_of(lax.rem(zl - way * dz + NZL, NZL) * shard, 16)
            pairs.append((ref.at[pl.ds(n * shard, shard)], w_buf.at[from_core, pl.ds(start, shard)]))
    run_copies(pairs, sems)
    half = w_buf.shape[2] // 2
    keys = 2 * half
    for side in range(2):
        product = jnp.dot(h_buf[...], w_buf[side], preferred_element_type=F32)
        k, v = product[:, :half], product[:, half:]
        own_ref[:, side * half : (side + 1) * half] = k[:TOK]
        own_ref[:, keys + side * half : keys + (side + 1) * half] = v[:TOK]
        for n, ref in enumerate(backs):
            rows = slice((n + 1) * TOK, (n + 2) * TOK)
            high = k[rows].astype(BF)
            low = (k[rows] - high.astype(F32)).astype(BF)
            for i, value in enumerate((high, low, v[rows].astype(BF))):
                ref[:, i * keys + side * half : i * keys + (side + 1) * half] = value


def project(coords, hidden, peers, bundles):
    part = peers[0].shape[1]
    width = bundles[0].shape[1]
    back = jax.ShapeDtypeStruct((TOK, 3 * width), BF)
    return pl.pallas_call(
        project_kernel,
        out_shape=(jax.ShapeDtypeStruct((TOK, 2 * width), F32),) + (back,) * (NX - 1),
        in_specs=[SMEM] + [HBM] * (1 + len(peers) + len(bundles)),
        out_specs=(VMEM,) * NX,
        scratch_shapes=[
            pltpu.VMEM((NX * TOK, part), BF),
            pltpu.VMEM((2, part, width), BF),
            pltpu.SemaphoreType.DMA((NX + 2 * NZL,)),
        ],
        cost_estimate=pl.CostEstimate(flops=10**11, bytes_accessed=1000, transcendentals=0),
        name="project",
    )(coords, hidden, *peers, *bundles)


def pack_kernel(*refs):
    at = 0
    for ref in refs[:-1]:
        refs[-1][at : at + ref.shape[0]] = ref[...]
        at += ref.shape[0]


def pack(blocks, rank):
    return pl.pallas_call(
        pack_kernel,
        out_shape=jax.ShapeDtypeStruct((sum(a.shape[0] for a in blocks), *blocks[0].shape[1:]), BF),
        in_specs=[VMEM] * len(blocks),
        out_specs=VMEM,
        compiler_params=pltpu.CompilerParams(vmem_limit_bytes=SMALL_LIMIT),
        cost_estimate=pl.CostEstimate(flops=rank, bytes_accessed=1000, transcendentals=0),
        name="pack",
    )(*blocks)


def seen_tokens(mask_ref, fork_ref, block):
    count = jnp.clip(fork_ref[0] + 1 - block * TOK, 0, TOK)
    return jnp.where(mask_ref[0, block] == 1, count, 0)


def attention_kernel(stage, together_heads, coord_ref, mask_ref, fork_ref, q_ref, *refs):
    segment, carried = stage == 2, stage > 0
    if segment:
        (cos_ref, sin_ref, gain_ref, own_ref), refs = refs[:4], refs[4:]
        backs, refs = refs[: NX - 1], refs[NX - 1 :]
    elif stage == 0:
        blocks, refs = [*(refs[0].at[n] for n in range(NY)), *refs[1 : NY + 1]], refs[NY + 1 :]
    else:
        blocks, refs = [refs[0].at[n] for n in range(2 * NY)], refs[1:]
    if carried:
        (acc_in, top_in, total_in), refs = refs[:3], refs[3:]
    if segment:
        out_ref, refs = refs[0], refs[1:]
    else:
        (acc_ref, top_ref, total_ref), refs = refs[:3], refs[3:]
    k_buf, v_buf = refs
    groups = k_buf.shape[0]
    heads = q_ref.shape[1] // HEAD
    per_group = heads // groups

    def lanes_of(h):
        return slice(h * HEAD, (h + 1) * HEAD)

    for g in range(groups):
        v_buf[g, :, HEAD:] = jnp.ones((k_buf.shape[1], HEAD), BF)
        if segment:
            k, v = own_ref[:, lanes_of(g)], own_ref[:, lanes_of(groups + g)]
            for ref in backs:
                high, low = ref[:, lanes_of(g)], ref[:, lanes_of(groups + g)]
                k = k + (high.astype(F32) + low.astype(F32))
                v = v + ref[:, lanes_of(2 * groups + g)].astype(F32)
            k = k * lax.rsqrt(jnp.mean(k * k, axis=1, keepdims=True) + EPS) * gain_ref[...]
            k = k * cos_ref[...] + pltpu.roll(k, HEAD // 2, 1) * sin_ref[...]
            k_buf[g] = k.astype(BF)
            v_buf[g, :, :HEAD] = v.astype(BF)
        else:
            for i, ref in enumerate(blocks):
                rows = slice(i * TOK, (i + 1) * TOK)
                k_buf[g, rows, :] = ref[0, :, lanes_of(g)]
                v_buf[g, rows, :HEAD] = ref[1, :, lanes_of(g)]
    if segment:
        row = lax.broadcasted_iota(jnp.int32, (TOK, TOK), 0)
        column = lax.broadcasted_iota(jnp.int32, (TOK, TOK), 1)
        bias = jnp.where(row >= column, 0.0, FLOOR)
        bias = jnp.concatenate([bias] * together_heads, axis=0)
    else:
        core, y, zh = coord_ref[CORE], coord_ref[Y], coord_ref[ZH]
        from_core = core if stage == 0 else 1 - core
        lane = lax.broadcasted_iota(jnp.int32, (1, TOK), 1)
        bias = []
        for side in (zh, 1 - zh):
            for away in ROUND_Y:
                block = lax.rem(y - away + NY, NY) * 4 + side * 2 + from_core
                bias.append(jnp.where(lane < seen_tokens(mask_ref, fork_ref, block), 0.0, FLOOR))
        bias = jnp.concatenate(bias, axis=1)
    units = [range(h, h + together_heads) for h in range(0, heads, together_heads)]

    def score(unit):
        q = jnp.concatenate([q_ref[:, lanes_of(h)] for h in unit], axis=0)
        return dot_nt(q, k_buf[unit[0] // per_group])

    ahead = score(units[0])
    for n, unit in enumerate(units):
        scores = ahead + bias
        if n + 1 < len(units):
            ahead = score(units[n + 1])
        top = jnp.max(scores, axis=1, keepdims=True)
        if carried:
            old = jnp.concatenate([top_in[:, lanes_of(h)] for h in unit], axis=0)
            wide = jnp.maximum(old, top)
            factor = jnp.exp2((old - wide) * EXP_SCALE)
            top = jnp.concatenate([wide] * (scores.shape[1] // HEAD), axis=1)
        else:
            wide = jnp.broadcast_to(top, (top.shape[0], HEAD))
        weights = jnp.exp2((scores - top) * EXP_SCALE).astype(BF)
        summed = jnp.dot(weights, v_buf[unit[0] // per_group], preferred_element_type=F32)
        for i, h in enumerate(unit):
            rows = slice(i * TOK, (i + 1) * TOK)
            value, total = summed[rows, :HEAD], summed[rows, HEAD:]
            if carried:
                value = value + acc_in[:, lanes_of(h)] * factor[rows]
                total = total + total_in[:, lanes_of(h)] * factor[rows]
            if segment:
                out_ref[:, lanes_of(h)] = (value / total).astype(BF)
            else:
                acc_ref[:, lanes_of(h)] = value
                top_ref[:, lanes_of(h)] = wide[rows]
                total_ref[:, lanes_of(h)] = total


def attention(stage, coords, mask, fork, queries, groups, operands):
    width = queries.shape[1]
    heads = width // HEAD
    length = TOK if stage == 2 else 2 * NY * TOK
    if stage == 2:
        out_shape = jax.ShapeDtypeStruct((TOK, width), BF)
    else:
        out_shape = (jax.ShapeDtypeStruct((TOK, width), F32),) * 3
    return pl.pallas_call(
        functools.partial(attention_kernel, stage, 4 if stage == 2 else 2),
        out_shape=out_shape,
        in_specs=[SMEM] * 3 + [VMEM] * (1 + len(operands)),
        out_specs=VMEM if stage == 2 else (VMEM,) * 3,
        scratch_shapes=[
            pltpu.VMEM((groups, length, HEAD), BF),
            pltpu.VMEM((groups, length, 2 * HEAD), BF),
        ],
        compiler_params=pltpu.CompilerParams(vmem_limit_bytes=VMEM_LIMIT),
        cost_estimate=pl.CostEstimate(flops=10**9, bytes_accessed=1000, transcendentals=0),
        name=("own_blocks", "other_blocks", "segment_block")[stage],
    )(coords, mask, fork, queries, *operands)


def on_device(
    hidden,
    queries,
    key_value_weight,
    k_gain,
    cached_ancestor_keys,
    cached_ancestor_values,
    ancestor_mask,
    fork_offset,
):
    dp, leaf = lax.axis_index("dp"), lax.axis_index("leaf")
    coords = jnp.stack([leaf % 2, leaf // 4, (leaf // 2) % 2, dp // NZL, dp % NZL]).astype(jnp.int32)
    groups = cached_ancestor_keys.shape[3] // HEAD
    keys, values = cached_ancestor_keys[0, 0], cached_ancestor_values[0, 0]
    load = pick_load(coords, key_value_weight, keys, values)
    unit = pick_unit(load)

    block_start = jnp.arange(ancestor_mask.shape[1], dtype=jnp.int32) * TOK
    seen = jnp.clip(fork_offset[:, None] + 1 - block_start[None, :], 0, TOK)
    start = jnp.sum(jnp.where(ancestor_mask == 1, seen, 0))
    positions = (start + jnp.arange(TOK, dtype=jnp.int32)).astype(F32)
    freq = THETA ** (-jnp.arange(HEAD // 2, dtype=F32) * 2.0 / HEAD)
    angle = positions[:, None] * freq
    cosine, sine = jnp.cos(angle), jnp.sin(angle)
    cosine = jnp.concatenate([cosine, cosine], axis=-1)
    sine = jnp.concatenate([-sine, sine], axis=-1)

    def direct(a, **by):
        return move(a, ways=(1, 1), **by)

    def to_y_peers(a):
        return [direct(a, y=n) for n in ROUND_Y[1:]]

    shard = key_value_weight.shape[0]
    got = move(load, z=4)
    fours = jnp.concatenate([load[:shard], got[:shard]], axis=0)
    fours, far, *near = together(fours, got[shard:].reshape(unit.shape), *to_y_peers(unit))
    sent = pick_parts(coords, got, hidden[0])
    far, two, part_two, part_one, part_three, cosine, sine = together(
        move(far, z=4), move(fours, z=2), *(direct(sent[n - 1], x=n) for n in (2, 1, 3)), cosine, sine
    )
    first = jnp.concatenate([fours, two], axis=0)
    second, other_first = together(move(first, z=1), swap_cores(first))
    other_second = swap_cores(second)
    peers = [part_one, part_two, part_three]
    partial, *backs = project(coords, hidden[0], peers, [first, second, other_first, other_second])
    backs = [direct(backs[n - 1], x=-n) for n in (2, 3, 1)]
    near = pack([unit, *near], 10**13)
    far = [far, *to_y_peers(far)]
    other = swap_cores(pack([near, *far], 10**6)).reshape(2 * NY, *unit.shape)
    blocks = [near.reshape(NY, *unit.shape), *far]

    given = (coords, ancestor_mask, fork_offset, queries[0], groups)
    state = attention(0, *given, blocks)
    state = attention(1, *given, [other, *state])
    result = attention(2, *given, [cosine, sine, k_gain[None, :], partial, *backs, *state])
    return result[None]


def solution(mesh):
    in_specs = (
        P(("dp", "leaf"), None, None),
        P(("dp", "leaf"), None, None),
        P("dp", None),
        P(),
        P("dp", "leaf", None, None),
        P("dp", "leaf", None, None),
        P(("dp", "leaf"), None),
        P(("dp", "leaf")),
    )
    out_specs = P(("dp", "leaf"), None, None)
    return jax.shard_map(
        on_device, mesh=mesh, in_specs=in_specs, out_specs=out_specs, check_vma=False
    )
```
